128 devices in a mesh: section: 32 (over z, y_lo, x), tensor: 4 (over y_hi, core).
Axes of the slice: x: 4, y: 4 (y_hi: 2, y_lo: 2; y = y_hi * 2 + y_lo), z: 4, core: 2. Of those that a mesh axis runs over, the one named last changes fastest.
Arguments:
- hidden: bfloat16 [512, 12288], P('section', 'tensor'), may hold values from -8 to 8, as said below
- embedding: bfloat16 [51200, 12288], P('section', 'tensor'), may hold values from -1 to 1, as said below
- bottom_grad: bfloat16 [512, 12288], P('section', 'tensor'), may hold values from -6 to 6
- targets: int32 [512], P('section'), may hold values from 0 to 51199
- token_ids: int32 [512], P('section'), may hold values from 0 to 51199
Outputs:
- input_grad: bfloat16 [512, 12288], P('section', 'tensor')
- table_grad: bfloat16 [51200, 12288], P('section', 'tensor')
The draws below stay inside these ranges and needn't reach their ends.
Inputs may be any that keep to these rules, and one draw needn't show every extreme that they name: `hidden`: activations of order one. `embedding`: entries of order 3 / sqrt(12288).
All inputs are finite; a program needn't handle non-finite values.
Results may differ from the reference program's by a relative error of at most 0.0026.
Values may be sent and summed in bfloat16 or wider, within the bound.
No kernel may reach another device: no remote copies, remote signals or barrier semaphores. Data moves between devices by JAX's collectives and lax.ppermute only.
A program may use at most 128 MiB of HBM per device.

```python
import math
import jax
import jax.numpy as jnp
import numpy as np
from jax import lax

D = 12288
VOCAB = 51200
TOKENS = 512


def embed_rows(key, row_ids):

    def one_row(index):
        return jax.random.normal(jax.random.fold_in(key, index), (D,), jnp.float32)
    return jax.vmap(one_row)(row_ids) * (3.0 / math.sqrt(D))


def draw_embedding(key, part):
    table = embed_rows(key, jnp.arange(VOCAB, dtype=jnp.int32))
    return jnp.clip(table, -1.0, 1.0).astype(jnp.bfloat16)


def draw_hidden(key, part):
    key = jax.random.fold_in(key, 5)
    values = jax.random.normal(key, (TOKENS, D), jnp.float32)
    return jnp.clip(values, -8.0, 8.0).astype(jnp.bfloat16)


def with_ends(values, key, least, high):
    spot = [jax.random.randint(jax.random.fold_in(key, axis), (), 0, length) for axis, length in enumerate(values.shape)]
    main_axis = values.shape.index(max(values.shape))
    beside = spot[:main_axis] + [(spot[main_axis] + 1) % values.shape[main_axis]] + spot[main_axis + 1:]
    return values.at[tuple(spot)].set(least).at[tuple(beside)].set(high)


def shard_levels(stream_key, dims, shards, least, high):
    def one(dim, shards_of):
        steps = jax.random.uniform(jax.random.fold_in(jax.random.fold_in(stream_key, 6), dim), (shards_of,), jnp.float32, least / len(shards), high / len(shards))
        return jnp.repeat(jnp.exp(steps), dims[dim] // shards_of).reshape((-1,) + (1,) * (len(dims) - dim - 1))

    level = one(*shards[0])
    for cut in shards[1:]:
        level = level * one(*cut)
    return level


def rank_table(count, skew):
    loads = [(1 << 20) // math.isqrt(standing ** skew) + 1 for standing in range(1, count + 1)]
    scale = 1 + sum(loads) // (1 << 30)
    return np.cumsum(np.array([max(1, weight // scale) for weight in loads]))


def ranked(rng, dims, amount, skew):
    listing = rank_table(amount, skew)
    ticket = jax.random.randint(jax.random.fold_in(rng, 1), dims, 0, int(listing[amount - 1]))
    rank = jnp.searchsorted(jnp.asarray(listing, jnp.int32), ticket, side="right")
    return jax.random.permutation(jax.random.fold_in(rng, 2), amount)[rank].astype(jnp.int32)


def bell_draw(key, dims, spread, most, cuts=(), kind=jnp.bfloat16):
    level = shard_levels(key, dims, cuts, -0.22, 0.18) if cuts else 1.0
    drawn = jax.random.normal(key, dims, jnp.float32) * spread * level
    return jnp.minimum(jnp.maximum(drawn, -most), most).astype(kind)


def setup_inputs(seed: int = 0) -> dict:
    streams_of = jax.random.split(jax.random.key(seed), 6)
    return {
        "hidden": draw_hidden(jax.random.fold_in(streams_of[5], 71), 0),
        "embedding": draw_embedding(jax.random.fold_in(streams_of[5], 71), 0),
        "bottom_grad": bell_draw(streams_of[2], (TOKENS, D), 1.0, 6.0, ((0, 32), (1, 4))),
        "targets": with_ends(jax.random.randint(streams_of[3], (TOKENS,), 0, VOCAB), jax.random.fold_in(streams_of[3], 1), 0, VOCAB - 1).astype(jnp.int32),
        "token_ids": with_ends(ranked(streams_of[4], (TOKENS,), VOCAB, 2), jax.random.fold_in(streams_of[4], 3), 0, VOCAB - 1).astype(jnp.int32),
    }


def reference(hidden, embedding, bottom_grad, targets, token_ids):
    logits = lax.dot_general(hidden, embedding, (((1,), (1,)), ((), ())), preferred_element_type=jnp.float32)
    maximum = jnp.max(logits, axis=1, keepdims=True)
    scaled = jnp.exp(logits - maximum)
    denominator = jnp.sum(scaled, axis=1, keepdims=True)
    probs = (scaled / denominator).astype(jnp.bfloat16)
    target_rows = embedding[targets].astype(jnp.float32)
    input_grad = (jnp.dot(probs, embedding, preferred_element_type=jnp.float32) - target_rows).astype(jnp.bfloat16)
    head_term = lax.dot_general(probs, hidden, (((0,), (0,)), ((), ())), preferred_element_type=jnp.float32)
    lookup_term = jnp.zeros((VOCAB, D), jnp.float32).at[token_ids].add(bottom_grad.astype(jnp.float32))
    lookup_term = lookup_term.at[targets].add(-hidden.astype(jnp.float32))
    table_grad = (head_term + lookup_term).astype(jnp.bfloat16)
    return input_grad, table_grad
```

```python
import jax
import jax.numpy as jnp
from jax import lax
from jax.sharding import PartitionSpec as P

BF16, F16, F32 = jnp.bfloat16, jnp.float16, jnp.float32
BOTH = ("section", "tensor")
SCALE = 16384.0


def linear(z, yl, x, yh, c):
    return (((z * 2 + yl) * 4 + x) * 2 + yh) * 2 + c


def permute(value, move):
    pairs = []
    for z in range(4):
        for yl in range(2):
            for x in range(4):
                for yh in range(2):
                    for c in range(2):
                        pairs.append((linear(z, yl, x, yh, c), linear(*move(z, yl, x, yh, c))))
    return lax.ppermute(value, BOTH, pairs)


def swap_y(value):
    return permute(value, lambda z, yl, x, yh, c: (z, 1 - yl, x, yh, c))


def swap_core(value):
    return permute(value, lambda z, yl, x, yh, c: (z, yl, x, yh, 1 - c))


def swap_half(value):
    return permute(value, lambda z, yl, x, yh, c: (z, yl, x, 1 - yh, c))


def ring_a(value, k):
    return permute(
        value,
        lambda z, yl, x, yh, c: ((z + k) % 4, yl, x, yh, c) if c == 0 else (z, yl, (x + k) % 4, yh, c),
    )


def ring_b(value, k):
    return permute(
        value,
        lambda z, yl, x, yh, c: (z, yl, (x + k) % 4, yh, c) if c == 0 else ((z + k) % 4, yl, x, yh, c),
    )


def put(buffer, block, index, dim):
    return lax.dynamic_update_slice_in_dim(buffer, jnp.expand_dims(block, dim), index, dim)


def pick(buffer, index, dim):
    return lax.dynamic_index_in_dim(buffer, index, dim, keepdims=False)


def place():
    section, tensor = lax.axis_index("section"), lax.axis_index("tensor")
    z, yl, x, c = section // 8, (section // 4) % 2, section % 4, tensor % 2
    first = jnp.where(c == 0, z, x)
    second = jnp.where(c == 0, x, z)
    return (yl + c) % 2, first, second


def gather_rows(own, cut, where):
    slot, first, second = where
    rows, cols = own.shape
    other = swap_y(own)
    pair = jnp.where(slot == 0, jnp.stack([own, other]), jnp.stack([other, own]))
    line = put(jnp.zeros((2, 4, rows, cols), own.dtype), pair, first, 1)
    for k in (1, 3, 2):
        line = put(line, ring_a(pair, k), (first - k) % 4, 1)
    parts = [(line, second)] + [(ring_b(line, k), (second - k) % 4) for k in (1, 3, 2)]
    main = jnp.zeros((2, 4, 4, rows, cut), own.dtype)
    rest = jnp.zeros((2, 4, 4, rows, cols - cut), own.dtype)
    for block, index in parts:
        main = put(main, block[..., :cut], index, 1)
        rest = put(rest, block[..., cut:], index, 1)
    return main, rest


def scatter_sum(value, where):
    slot, first, second = where

    def ring(total, index, shift):
        out = pick(total, index, 1)
        for k in (1, 3, 2):
            out = out + shift(pick(total, (index + k) % 4, 1).astype(F16), k).astype(F32)
        return out

    line = ring(value, second, ring_b)
    pair = ring(line, first, ring_a)
    return pick(pair, slot, 0) + swap_y(pick(pair, 1 - slot, 0).astype(F16)).astype(F32)


def body(hidden, embedding, bottom_grad, targets, token_ids):
    rows, width = hidden.shape
    vocab_rows = embedding.shape[0]
    vocab_first = lax.axis_index("section") * vocab_rows
    where = place()
    digits = jnp.stack([targets // 256, targets % 256, token_ids // 256, token_ids % 256], axis=1)
    digits = jnp.pad(digits.astype(BF16), ((0, 0), (0, 124)))
    hid, codes = gather_rows(jnp.concatenate([hidden, digits], axis=1), width, where)
    tokens = 32 * rows
    codes = codes.reshape(tokens, 128)[:, :4].astype(jnp.int32)
    target_all = codes[:, 0] * 256 + codes[:, 1]
    ids_all = codes[:, 2] * 256 + codes[:, 3]

    bottom_grad, _ = lax.optimization_barrier((bottom_grad, hid[0, 0, 0, 0, :8]))
    bottom_all, _ = gather_rows(bottom_grad, width, where)

    half = tokens // 2
    dims = (((1,), (1,)), ((), ()))
    sent = lax.dot_general(hid[1].reshape(half, width), embedding, dims, preferred_element_type=F32)
    kept = lax.dot_general(hid[0].reshape(half, width), embedding, dims, preferred_element_type=F32)
    got = swap_core(sent).reshape(4, 4, rows, vocab_rows).transpose(1, 0, 2, 3).reshape(half, vocab_rows)
    partial = kept + got
    logits = partial + swap_half(partial.astype(F16)).astype(F32)

    local_max = jnp.max(logits, axis=1)
    local_sum = jnp.sum(jnp.exp(logits - local_max[:, None]), axis=1)
    stats = jnp.stack([local_max, local_sum]).reshape(1, 2, half)
    stats = lax.all_to_all(jnp.broadcast_to(stats, (32, 2, half)), "section", 0, 0, tiled=True)
    maximum = jnp.max(stats[:, 0], axis=0)
    denominator = jnp.sum(stats[:, 1] * jnp.exp(stats[:, 0] - maximum), axis=0)
    probs_kept = (jnp.exp(logits - maximum[:, None]) / denominator[:, None]).astype(BF16)
    probs_got = swap_core(probs_kept).reshape(4, 4, rows, vocab_rows).transpose(1, 0, 2, 3).reshape(half, vocab_rows)
    probs = jnp.concatenate([probs_kept, probs_got], axis=0)

    columns = jnp.arange(vocab_rows, dtype=jnp.int32)
    wanted = target_all - vocab_first
    inside = ((wanted >= 0) & (wanted < vocab_rows)).astype(F32)
    picked = jnp.take(embedding, jnp.clip(wanted, 0, vocab_rows - 1), axis=0).astype(F32)
    value = jnp.dot(probs, embedding, preferred_element_type=F32) - picked * inside[:, None]
    value = (value * SCALE).reshape(2, 4, 4, rows, width)
    input_grad = (scatter_sum(value, where) * (1.0 / SCALE)).astype(BF16)

    all_ids = jnp.concatenate([ids_all, target_all], axis=0)
    id_hits = (all_ids[:, None] - vocab_first == columns[None, :]).astype(BF16)
    hidden_all = hid.reshape(tokens, width)
    lookup_rows = jnp.concatenate([bottom_all.reshape(tokens, width), -hidden_all], axis=0)
    contract = (((0,), (0,)), ((), ()))
    head_term = lax.dot_general(probs, hidden_all, contract, preferred_element_type=F32)
    lookup_term = lax.dot_general(id_hits, lookup_rows, contract, preferred_element_type=F32)
    table_grad = (head_term + lookup_term).astype(BF16)
    return (input_grad, table_grad)


def solution(mesh):
    split = P("section", "tensor")
    in_specs = (split, split, split, P("section"), P("section"))
    return jax.shard_map(body, mesh=mesh, in_specs=in_specs, out_specs=(split, split), check_vma=False)
```

```python
import functools

import jax
import jax.numpy as jnp
from jax import lax
from jax.experimental import pallas as pl
from jax.experimental.pallas import tpu as pltpu
from jax.sharding import PartitionSpec as P

BF16, F16, F32, I32 = jnp.bfloat16, jnp.float16, jnp.float32, jnp.int32
BOTH = ("section", "tensor")
SCALE = 16384.0
VMEM = 24 * 1024 * 1024
LARGE = 50 * 1024 * 1024
ROWS = 16
CHUNK = 256
TOKENS = 512
MANY = 128
ANY = pl.BlockSpec(memory_space=pl.ANY)
NEAR = pl.BlockSpec(memory_space=pltpu.VMEM)


def linear(z, yl, x, yh, c):
    return (((z * 2 + yl) * 4 + x) * 2 + yh) * 2 + c


def permute(value, move):
    pairs = []
    for z in range(4):
        for yl in range(2):
            for x in range(4):
                for yh in range(2):
                    for c in range(2):
                        pairs.append((linear(z, yl, x, yh, c), linear(*move(z, yl, x, yh, c))))
    return lax.ppermute(value, BOTH, pairs)


def swap_y(value):
    return permute(value, lambda z, yl, x, yh, c: (z, 1 - yl, x, yh, c))


def swap_core(value):
    return permute(value, lambda z, yl, x, yh, c: (z, yl, x, yh, 1 - c))


def swap_half(value):
    return permute(value, lambda z, yl, x, yh, c: (z, yl, x, 1 - yh, c))


def ring_a(value, k):
    return permute(
        value,
        lambda z, yl, x, yh, c: ((z + k) % 4, yl, x, yh, c) if c == 0 else (z, yl, (x + k) % 4, yh, c),
    )


def ring_b(value, k):
    return permute(
        value,
        lambda z, yl, x, yh, c: (z, yl, (x + k) % 4, yh, c) if c == 0 else ((z + k) % 4, yl, x, yh, c),
    )


def gather_rows(own, bottom):
    both = jnp.stack([own, bottom])
    lines = jnp.stack([both] + [ring_a(both, k) for k in (1, 2, 3)], axis=1)
    line, bottom = lines[0], lines[1]
    other = swap_y(line)
    later = jnp.where(other[0, 0, -128] >= 0, line, 0)
    mine = [line, ring_b(line, 1), ring_b(later, 2), ring_b(line, 3)]
    chunks = [mine, [other] + [ring_b(other, k) for k in (1, 2, 3)]]
    return chunks, (bottom, swap_y(bottom))


def gather_rest(lines, ready):
    line = jnp.where(ready, jnp.concatenate(lines), 0)
    parts = [line] + [ring_b(line, k) for k in (1, 2, 3)]
    return [part.reshape(8 * ROWS, part.shape[-1]) for part in parts]


def ring_sum(total, shift):
    total = total.astype(F16)
    parts = [shift(total[k], -k).astype(F32) for k in (1, 2, 3)]
    return total[0].astype(F32) + parts[0] + parts[1] + parts[2]


ORDER = [(2 * m + par, j) for par in range(2) for m in range(2) for j in range(4)]


def fetch_rows(core, pieces, rows, first, done):
    width = rows.shape[1]

    def start(n, piece, j):
        source = piece.at[j, :, pl.ds(0, width)]
        pltpu.make_async_copy(source, rows.at[pl.ds(first + ROWS * n, ROWS), :], done.at[n]).start()

    @pl.when(core == 0)
    def _():
        for n, (i, j) in enumerate(ORDER):
            start(n, pieces[i], j)

    @pl.when(core != 0)
    def _():
        for n, (i, j) in enumerate(ORDER):
            start(n, pieces[j], i)


def await_rows(pieces, rows, first, done):
    width = rows.shape[1]
    for n in range(len(ORDER)):
        source = pieces[0].at[0, :, pl.ds(0, width)]
        pltpu.make_async_copy(source, rows.at[pl.ds(first + ROWS * n, ROWS), :], done.at[n]).wait()


def logits_kernel(flags, *refs):
    pieces, (table, kept, sent, out, rows, turned, tiles, done, left, arrived) = refs[:8], refs[8:]
    step, half = table.shape[0] // 4, CHUNK // 2
    parts = [pl.ds(step * n, step) for n in range(4)]
    copies = [pltpu.make_async_copy(table.at[p, :], tiles.at[p, :], arrived.at[n]) for n, p in enumerate(parts)]
    for c in range(2):
        fetch_rows(flags[0], pieces[4 * c : 4 * c + 4], rows, CHUNK * c, done.at[c])
    for tile in copies:
        tile.start()
    for c in range(2):
        await_rows(pieces[4 * c : 4 * c + 4], rows, CHUNK * c, done.at[c])
    copy = pltpu.make_async_copy(rows, out, left.at[0])
    copy.start()
    turned[...] = rows[...].T
    even = flags[1] == 0
    for n in range(4):
        copies[n].wait()
        part = slice(step * n, step * (n + 1))
        product = jnp.dot(tiles[part, :], turned[...], preferred_element_type=F32)
        for c in range(2):
            lanes = slice(half * c, half * (c + 1))
            low = product[:, CHUNK * c : CHUNK * c + half]
            high = product[:, CHUNK * c + half : CHUNK * (c + 1)]
            kept[part, lanes] = jnp.where(even, low, high)
            sent[part, lanes] = jnp.where(even, high, low)
    copy.wait()


def logits_part(flags, chunks, table):
    vocab, width = table.shape
    return pl.pallas_call(
        logits_kernel,
        grid_spec=pltpu.PrefetchScalarGridSpec(
            num_scalar_prefetch=1,
            grid=(),
            in_specs=[ANY] * 9,
            out_specs=[NEAR, NEAR, ANY],
            scratch_shapes=[
                pltpu.VMEM((TOKENS, width), BF16),
                pltpu.VMEM((width, TOKENS), BF16),
                pltpu.VMEM((vocab, width), BF16),
                pltpu.SemaphoreType.DMA((2, len(ORDER))),
                pltpu.SemaphoreType.DMA((1,)),
                pltpu.SemaphoreType.DMA((4,)),
            ],
        ),
        out_shape=[jax.ShapeDtypeStruct((vocab, CHUNK), F32)] * 2 + [jax.ShapeDtypeStruct((TOKENS, width), BF16)],
        compiler_params=pltpu.CompilerParams(vmem_limit_bytes=LARGE),
        cost_estimate=pl.CostEstimate(flops=2 * TOKENS * vocab * width, bytes_accessed=16 << 20, transcendentals=0),
    )(flags, *chunks[0], *chunks[1], table)


def turning(flags):
    place = lax.broadcasted_iota(I32, (CHUNK, CHUNK), 0)
    step = lax.broadcasted_iota(I32, (CHUNK, CHUNK), 1)
    y = (step // 128 + flags[2]) % 2
    x = (flags[3] + 2 - step // 64 % 2) % 2
    z = (flags[4] + 4 - step // 16 % 4) % 4
    return (place == y * 128 + x * 64 + z * 16 + step % 16).astype(F32)


def turn(flags, rows):
    both = jnp.concatenate(rows + [jnp.zeros((8 - len(rows), CHUNK), F32)], axis=0)
    return jnp.dot(both, turning(flags), precision=lax.Precision.HIGHEST, preferred_element_type=F32)


def stats_kernel(flags, logits, after, stats):
    del after
    top = jnp.max(logits[...], axis=0, keepdims=True)
    total = jnp.sum(jnp.exp(logits[...] - top), axis=0, keepdims=True)
    placed = turn(flags, [top, total])
    for n in range(32):
        stats[n] = placed[0:2]


def stats_part(flags, logits, after):
    return pl.pallas_call(
        stats_kernel,
        grid_spec=pltpu.PrefetchScalarGridSpec(
            num_scalar_prefetch=1, grid=(), in_specs=[NEAR, ANY], out_specs=NEAR
        ),
        out_shape=jax.ShapeDtypeStruct((32, 2, CHUNK), F32),
        compiler_params=pltpu.CompilerParams(vmem_limit_bytes=VMEM),
        cost_estimate=pl.CostEstimate(flops=1 << 20, bytes_accessed=2 << 20, transcendentals=logits.size),
    )(flags, logits, after)


def probs_kernel(flags, stats, logits, after0, after1, after2, probs):
    del after0, after1, after2
    top = jnp.max(stats[:, 0, :], axis=0, keepdims=True)
    total = jnp.sum(stats[:, 1, :] * jnp.exp(stats[:, 0, :] - top), axis=0, keepdims=True)
    both = turn(flags, [top, total])
    probs[...] = (jnp.exp(logits[...] - both[0:1]) / both[1:2]).astype(BF16)


def probs_part(flags, stats, logits, after):
    return pl.pallas_call(
        probs_kernel,
        grid_spec=pltpu.PrefetchScalarGridSpec(
            num_scalar_prefetch=1, grid=(), in_specs=[NEAR, NEAR, ANY, ANY, ANY], out_specs=NEAR
        ),
        out_shape=jax.ShapeDtypeStruct(logits.shape, BF16),
        compiler_params=pltpu.CompilerParams(vmem_limit_bytes=VMEM),
        cost_estimate=pl.CostEstimate(flops=1 << 20, bytes_accessed=3 << 20, transcendentals=logits.size),
    )(flags, stats, logits, *after)


def ranks(by_lane, by_row, vocab):
    count = by_row.shape[0]
    lane_in = ((by_lane >= 0) & (by_lane < vocab)).astype(F32)
    row_in = ((by_row >= 0) & (by_row < vocab)).astype(F32)
    row = lax.broadcasted_iota(I32, (count, count), 0)
    lane = lax.broadcasted_iota(I32, (count, count), 1)
    lane_rank = jnp.sum(jnp.where(row < lane, row_in, 0.0), axis=0, keepdims=True).astype(I32)
    row_rank = jnp.sum(jnp.where(lane < row, lane_in, 0.0), axis=1, keepdims=True).astype(I32)
    return (
        jnp.where(lane_in > 0.0, lane_rank, -1),
        jnp.where(row_in > 0.0, row_rank, -1),
        jnp.sum(lane_in).astype(I32),
    )


def write_blocks(core, value, out, columns=slice(None), less=None):
    def write(c, n, i, j):
        rows = value[CHUNK * c + ROWS * n : CHUNK * c + ROWS * (n + 1)]
        if less is not None:
            rows = (rows - less[i, c, j, :, columns].astype(F32)) * SCALE
        out[i, c, j, :, columns] = rows

    @pl.when(core == 0)
    def _():
        for c in range(2):
            for n, (i, j) in enumerate(ORDER):
                write(c, n, i, j)

    @pl.when(core != 0)
    def _():
        for c in range(2):
            for n, (i, j) in enumerate(ORDER):
                write(c, n, j, i)


def target_kernel(flags, table, by_lane, by_row, after, out, lane_rank, row_rank, rows, tokens, hits):
    del after
    vocab = table.shape[0]

    def picks(first):
        slot = first + lax.broadcasted_iota(I32, (MANY, TOKENS), 0)
        found = jnp.sum(jnp.where(lane_rank[...] == slot, by_lane[...], 0), axis=1, keepdims=True)
        rows = (lax.broadcasted_iota(I32, (MANY, vocab), 1) == found).astype(F32).astype(BF16)
        slot = first + lax.broadcasted_iota(I32, (TOKENS, MANY), 1)
        return rows, (row_rank[...] == slot).astype(F32).astype(BF16)

    lane, row, count = ranks(by_lane[...], by_row[...], vocab)
    lane_rank[...] = lane
    row_rank[...] = row
    hits[0] = count
    rows[...], tokens[...] = picks(0)

    @pl.loop(0, table.shape[1] // 512)
    def _(n):
        columns = pl.ds(pl.multiple_of(n * 512, 512), 512)

        def spread_rows(rows, tokens):
            few = jnp.dot(rows, table[:, columns], preferred_element_type=F32).astype(BF16)
            return jnp.dot(tokens, few, preferred_element_type=F32)

        value = spread_rows(rows[...], tokens[...])
        write_blocks(flags[0], value.astype(BF16), out, columns)

        @pl.when(hits[0] > MANY)
        def _():
            def more(n, total):
                return total + spread_rows(*picks(n * MANY))

            value = lax.fori_loop(1, (hits[0] + MANY - 1) // MANY, more, spread_rows(rows[...], tokens[...]))
            write_blocks(flags[0], value.astype(BF16), out, columns)


def target_rows(flags, table, wanted, after):
    vocab, width = table.shape
    return pl.pallas_call(
        target_kernel,
        grid_spec=pltpu.PrefetchScalarGridSpec(
            num_scalar_prefetch=1,
            grid=(),
            in_specs=[NEAR, NEAR, NEAR, ANY],
            out_specs=NEAR,
            scratch_shapes=[
                pltpu.VMEM((1, TOKENS), I32),
                pltpu.VMEM((TOKENS, 1), I32),
                pltpu.VMEM((MANY, vocab), BF16),
                pltpu.VMEM((TOKENS, MANY), BF16),
                pltpu.SMEM((1,), I32),
            ],
        ),
        out_shape=jax.ShapeDtypeStruct((4, 2, 4, ROWS, width), BF16),
        compiler_params=pltpu.CompilerParams(vmem_limit_bytes=VMEM),
        cost_estimate=pl.CostEstimate(flops=512 * vocab * width, bytes_accessed=14 << 20, transcendentals=0),
    )(flags, table, wanted[None, :], wanted[:, None], after)


def input_kernel(flags, kept, got, table, picked, out, both, turned, left, done):
    half, step = CHUNK // 2, 512
    for n in range(2):
        mine = pl.multiple_of(n * CHUNK + flags[1] * half, half)
        other = pl.multiple_of(n * CHUNK + (1 - flags[1]) * half, half)
        lanes = slice(half * n, half * (n + 1))
        turned[:, pl.ds(mine, half)] = kept[:, lanes]
        turned[:, pl.ds(other, half)] = got[:, lanes]
    copy = pltpu.make_async_copy(turned, both, done.at[0])
    copy.start()
    left[...] = turned[...].T

    @pl.loop(0, table.shape[1] // step)
    def _(n):
        columns = pl.ds(pl.multiple_of(n * step, step), step)
        value = jnp.dot(left[...], table[:, columns], preferred_element_type=F32)
        write_blocks(flags[0], value, out, columns, picked)

    copy.wait()


def input_part(flags, table, kept, got, picked):
    vocab, width = table.shape
    return pl.pallas_call(
        input_kernel,
        grid_spec=pltpu.PrefetchScalarGridSpec(
            num_scalar_prefetch=1,
            grid=(),
            in_specs=[NEAR, NEAR, NEAR, NEAR],
            out_specs=[NEAR, ANY],
            scratch_shapes=[
                pltpu.VMEM((vocab, TOKENS), BF16),
                pltpu.VMEM((TOKENS, vocab), BF16),
                pltpu.SemaphoreType.DMA((1,)),
            ],
        ),
        out_shape=[
            jax.ShapeDtypeStruct((4, 2, 4, ROWS, width), F32),
            jax.ShapeDtypeStruct((vocab, TOKENS), BF16),
        ],
        compiler_params=pltpu.CompilerParams(vmem_limit_bytes=VMEM),
        cost_estimate=pl.CostEstimate(flops=1024 * vocab * width, bytes_accessed=16 << 20, transcendentals=0),
    )(flags, kept, got, table, picked)


def lookup_picks(first, vocab, lane_rank, row_rank, by_row):
    slot = first + lax.broadcasted_iota(I32, (MANY, 2 * TOKENS), 0)
    source = lax.broadcasted_iota(I32, (MANY, 2 * TOKENS), 1)
    sign = jnp.where(source < TOKENS, -1.0, 1.0)
    lie = jnp.where(lane_rank == slot, sign, 0.0).astype(BF16)
    slot = first + lax.broadcasted_iota(I32, (2 * TOKENS, MANY), 1)
    found = jnp.sum(jnp.where(row_rank == slot, by_row, 0), axis=0, keepdims=True)
    go = (lax.broadcasted_iota(I32, (vocab, MANY), 0) == found).astype(F32).astype(BF16)
    return lie, go


def lookup_kernel(flags, rows, b0, b1, b2, b3, c0, c1, c2, c3, near, far, few, go, lane_rank, row_rank, by_row, lie):
    @pl.when(pl.program_id(0) == 0)
    def _():
        vocab = go.shape[0]
        codes = [c[...].astype(F32) for c in (c0, c1, c2, c3)]
        lanes = [c.T for c in codes]
        lanes = [(c[0:1, :] * 256.0 + c[1:2, :]).astype(I32) - flags[5] for c in lanes]
        by_lane = jnp.concatenate([near[...]] + lanes, axis=1)
        by_row[0:TOKENS, :] = far[...]
        for n, c in enumerate(codes):
            ids = (c[:, 0:1] * 256.0 + c[:, 1:2]).astype(I32) - flags[5]
            by_row[TOKENS + 8 * ROWS * n : TOKENS + 8 * ROWS * (n + 1), :] = ids
        lane, row, _ = ranks(by_lane, by_row[...], vocab)
        lane_rank[...] = lane
        row_rank[...] = row
        lie[...], go[...] = lookup_picks(0, vocab, lane, row, by_row[...])

    few[...] = lookup_sum(lie[...], rows, (b0, b1, b2, b3)).astype(BF16)


def lookup_sum(lie, rows, bottom):
    total = 0.0
    first = 0
    for part in (rows, *bottom):
        total = total + jnp.dot(lie[:, first : first + part.shape[0]], part[...], preferred_element_type=F32)
        first += part.shape[0]
    return total


def lookup_rows(flags, rows, bottom, wanted, vocab):
    width = rows.shape[1]
    step = 1024 if width % 1024 == 0 else 512
    lane = pl.BlockSpec((1, 2 * TOKENS), lambda n, s: (0, 0))
    row = pl.BlockSpec((2 * TOKENS, 1), lambda n, s: (0, 0))
    return pl.pallas_call(
        lookup_kernel,
        grid_spec=pltpu.PrefetchScalarGridSpec(
            num_scalar_prefetch=1,
            grid=(width // step,),
            in_specs=[pl.BlockSpec((TOKENS, step), lambda n, s: (0, n))]
            + [pl.BlockSpec((8 * ROWS, step), lambda n, s: (0, n))] * 4
            + [pl.BlockSpec((8 * ROWS, 128), lambda n, s: (0, width // 128))] * 4
            + [pl.BlockSpec((1, TOKENS), lambda n, s: (0, 0)), pl.BlockSpec((TOKENS, 1), lambda n, s: (0, 0))],
            out_specs=[
                pl.BlockSpec((MANY, step), lambda n, s: (0, n)),
                pl.BlockSpec((vocab, MANY), lambda n, s: (0, 0)),
                lane,
                row,
                row,
            ],
            scratch_shapes=[pltpu.VMEM((MANY, 2 * TOKENS), BF16)],
        ),
        out_shape=[
            jax.ShapeDtypeStruct((MANY, width), BF16),
            jax.ShapeDtypeStruct((vocab, MANY), BF16),
            jax.ShapeDtypeStruct((1, 2 * TOKENS), I32),
            jax.ShapeDtypeStruct((2 * TOKENS, 1), I32),
            jax.ShapeDtypeStruct((2 * TOKENS, 1), I32),
        ],
        compiler_params=pltpu.CompilerParams(vmem_limit_bytes=VMEM),
        cost_estimate=pl.CostEstimate(flops=256 * 1024 * width, bytes_accessed=7 << 20, transcendentals=0),
    )(flags, rows, *bottom, *bottom, wanted[None, :], wanted[:, None])


def table_kernel(probs, rows, b0, b1, b2, b3, few, go, by_row, lane_rank, row_rank, out, order, total, hits):
    vocab = out.shape[0]

    @pl.when(pl.program_id(0) == 0)
    def _():
        order[...] = jnp.zeros_like(order)
        hits[0] = jnp.max(lane_rank[...].astype(F32)).astype(I32) + 1

    def first():
        value = jnp.dot(probs[...], rows[...], preferred_element_type=F32)
        return value + jnp.dot(go[...], few[...], preferred_element_type=F32)

    out[...] = first().astype(BF16)

    @pl.when(hits[0] > MANY)
    def _():
        total[...] = first()

        @pl.loop(1, (hits[0] + MANY - 1) // MANY)
        def _(n):
            lie, there = lookup_picks(n * MANY, vocab, lane_rank[...], row_rank[...], by_row[...])
            more = lookup_sum(lie, rows, (b0, b1, b2, b3)).astype(BF16)
            total[...] += jnp.dot(there, more, preferred_element_type=F32)

        out[...] = total[...].astype(BF16)


def table_part(probs, rows, bottom, prepared):
    few, go, lane_rank, row_rank, wanted = prepared
    vocab, width = probs.shape[0], few.shape[1]
    step = 512
    return pl.pallas_call(
        table_kernel,
        grid=(width // step,),
        in_specs=[pl.BlockSpec((vocab, TOKENS), lambda n: (0, 0))]
        + [pl.BlockSpec((TOKENS, step), lambda n: (0, n))]
        + [pl.BlockSpec((8 * ROWS, step), lambda n: (0, n))] * 4
        + [
            pl.BlockSpec((MANY, step), lambda n: (0, n)),
            pl.BlockSpec((vocab, MANY), lambda n: (0, 0)),
            pl.BlockSpec((2 * TOKENS, 1), lambda n: (0, 0)),
            pl.BlockSpec((1, 2 * TOKENS), lambda n: (0, 0)),
            pl.BlockSpec((2 * TOKENS, 1), lambda n: (0, 0)),
        ],
        out_specs=[
            pl.BlockSpec((vocab, step), lambda n: (0, n)),
            pl.BlockSpec((8, 128), lambda n: (0, 0)),
        ],
        scratch_shapes=[pltpu.VMEM((vocab, step), F32), pltpu.SMEM((1,), I32)],
        out_shape=[jax.ShapeDtypeStruct((vocab, width), BF16), jax.ShapeDtypeStruct((8, 128), F32)],
        compiler_params=pltpu.CompilerParams(vmem_limit_bytes=VMEM),
        cost_estimate=pl.CostEstimate(flops=2 * 640 * vocab * width, bytes_accessed=20 << 20, transcendentals=0),
    )(probs, rows, *bottom, few, go, wanted, lane_rank, row_rank)


def digits_of(ids):
    digits = jnp.stack([ids // 256, ids % 256], axis=1)
    return jnp.pad(digits.astype(BF16), ((0, 0), (0, 126)))


def ids_of(codes):
    codes = codes.astype(I32)
    return codes[..., 0] * 256 + codes[..., 1]


def body(hidden, embedding, bottom_grad, targets, token_ids):
    width = hidden.shape[1]
    vocab = embedding.shape[0]
    section, tensor = lax.axis_index("section"), lax.axis_index("tensor")
    vocab_first = section * vocab
    z, yl, x, core = section // 8, (section // 4) % 2, section % 4, tensor % 2
    odd = (x + core) % 2
    x_place = (x - odd - core) // 2
    flags = jnp.stack([core, odd, yl, x_place % 2, z, vocab_first]).astype(I32)

    hidden = jnp.concatenate([hidden, digits_of(targets)], axis=1)
    bottom = jnp.concatenate([bottom_grad, digits_of(token_ids)], axis=1)
    chunks, lines = gather_rows(hidden, bottom)

    def wanted_of(pieces):
        ids = ids_of(jnp.stack([p[..., width : width + 2] for p in pieces]))
        ids = jnp.where(core == 0, ids, ids.transpose(1, 0, 2))
        return ids.reshape(2, 2, 4, ROWS).transpose(1, 0, 2, 3).reshape(CHUNK) - vocab_first

    wanted = [wanted_of(pieces) for pieces in chunks]


    kept, sent, rows = logits_part(flags, chunks, embedding)
    partial = kept + swap_core(sent)
    logits = partial + swap_half(partial.astype(F16)).astype(F32)
    picked = target_rows(flags, embedding, jnp.concatenate(wanted), partial)

    bottom = gather_rest(lines, partial[0, 0] > -1e30)
    prepared = lookup_rows(flags, rows, bottom, jnp.concatenate(wanted), vocab)

    stats = lax.all_to_all(stats_part(flags, logits, picked), "section", 0, 0, tiled=True)
    mine = probs_part(flags, stats, logits, bottom[1:])
    value, probs = input_part(flags, embedding, mine, swap_core(mine), picked)
    line = ring_sum(value, ring_b)

    table_grad, zeros = table_part(probs, rows, bottom, prepared)
    line = line + zeros[0, 0]
    pair = ring_sum(line.transpose(1, 0, 2, 3), ring_a)
    input_grad = pair[0] + swap_y(pair[1].astype(F16)).astype(F32)
    return ((input_grad * (1.0 / SCALE)).astype(BF16), table_grad)


def solution(mesh):
    split = P("section", "tensor")
    in_specs = (split, split, split, P("section"), P("section"))
    return jax.shard_map(body, mesh=mesh, in_specs=in_specs, out_specs=(split, split), check_vma=False)
```
